32 devices in a mesh: groups: 2 (over y), tp: 4 (over z), sec: 2 (over x), dp: 2 (over core).
Axes of the slice: x: 2, y: 2, z: 4, core: 2. Of those that a mesh axis runs over, the one named last changes fastest.
Arguments:
- giant_context: bfloat16 [6144, 2048], P('tp', ('groups', 'sec', 'dp')), parts along dimension 1, may hold values from -40 to 40
- clip_context: bfloat16 [5120, 2048], P('tp', ('groups', 'sec', 'dp')), parts along dimension 1, may hold values from -40 to 40
- giant_out: bfloat16 [6144, 6144], P('tp'), may hold values from -1 to 1
- clip_out: bfloat16 [5120, 5120], P('tp'), may hold values from -1 to 1
- giant_gain: float32 [6144], P('tp'), may hold values from 0.5 to 1.5
- clip_gain: float32 [5120], P('tp'), may hold values from 0.5 to 1.5
- student_features: bfloat16 [2048, 1280], P(('groups', 'sec', 'dp')), parts along dimension 0, may hold values from -6 to 6
- giant_first: bfloat16 [1280, 1280], P('tp'), may hold values from -0.15625 to 0.15625
- clip_first: bfloat16 [1280, 1280], P('tp'), may hold values from -0.15625 to 0.15625
- giant_head: bfloat16 [6144, 1280], P('tp'), may hold values from -2 to 2
- clip_head: bfloat16 [5120, 1280], P('tp'), may hold values from -2 to 2
Outputs:
- giant_grad: bfloat16 [12288, 1280], P(('groups', 'tp'), ('sec', 'dp')), parts along dimension 0
- clip_grad: bfloat16 [10240, 1280], P(('groups', 'tp'), ('sec', 'dp')), parts along dimension 0
- giant_first_grad: bfloat16 [2560, 1280], P(('groups', 'tp'), ('sec', 'dp')), parts along dimension 0
- clip_first_grad: bfloat16 [2560, 1280], P(('groups', 'tp'), ('sec', 'dp')), parts along dimension 0
- feature_grad: bfloat16 [2048, 1280], P(('groups', 'sec', 'dp')), parts along dimension 0
The draws below stay inside these ranges and needn't reach their ends.
There are 2 independent parts, one for each index of `groups`. The reference program is written for one: setup_inputs(seed, part) draws one part's arguments, and reference() takes and returns one part's arrays. A program takes and returns all parts, laid end to end along the dimension named above; an argument that names none is the same for every part. Nothing has to cross between parts.
All inputs are finite; a program needn't handle non-finite values.
Results may differ from the reference program's by a relative error of at most 0.02.
Values may be sent and summed in bfloat16 or wider, within the bound.
A program may use at most 128 MiB of HBM per device.

```python
import math
import jax
import jax.numpy as jnp
from jax import lax

DG = 6144
DC = 5120
DS = 1280
DH = 1280
TOKENS = 1024
N_TP = 4


def draw_giant_context(key, part):
    key = jax.random.fold_in(key, 11)
    noise_key, scale_key = jax.random.split(key)
    base = jnp.clip(jax.random.normal(noise_key, (DG, TOKENS), jnp.float32), -4.0, 4.0)
    top = math.log(10.0)
    scale = jnp.exp(jax.random.uniform(scale_key, (1, TOKENS), jnp.float32, 0.0, top))
    return (base * scale).astype(jnp.bfloat16)


def draw_clip_context(key, part):
    key = jax.random.fold_in(key, 12)
    noise_key, scale_key = jax.random.split(key)
    base = jnp.clip(jax.random.normal(noise_key, (DC, TOKENS), jnp.float32), -4.0, 4.0)
    top = math.log(10.0)
    scale = jnp.exp(jax.random.uniform(scale_key, (1, TOKENS), jnp.float32, 0.0, top))
    return (base * scale).astype(jnp.bfloat16)


def draw_giant_out(key, part):
    key = jax.random.fold_in(key, 21)
    noise_key, scale_key = jax.random.split(key)
    base = jnp.clip(jax.random.normal(noise_key, (DG, DG), jnp.float32), -4.0, 4.0)
    trend = math.log(3.0)
    position = jnp.arange(DG, dtype=jnp.float32).reshape(1, DG) / (DG - 1)
    rough = jax.random.uniform(scale_key, (1, DG), jnp.float32, 0.0, math.log(4.0))
    scale = jnp.exp(trend * position + rough) / math.sqrt(DG)
    return jnp.clip(base * scale, -1.0, 1.0).astype(jnp.bfloat16)


def draw_clip_out(key, part):
    key = jax.random.fold_in(key, 22)
    noise_key, scale_key = jax.random.split(key)
    base = jnp.clip(jax.random.normal(noise_key, (DC, DC), jnp.float32), -4.0, 4.0)
    trend = math.log(3.0)
    position = jnp.arange(DC, dtype=jnp.float32).reshape(1, DC) / (DC - 1)
    rough = jax.random.uniform(scale_key, (1, DC), jnp.float32, 0.0, math.log(4.0))
    scale = jnp.exp(trend * position + rough) / math.sqrt(DC)
    return jnp.clip(base * scale, -1.0, 1.0).astype(jnp.bfloat16)


def draw_giant_head(key, part):
    key = jax.random.fold_in(key, 31)
    noise_key, scale_key = jax.random.split(key)
    base = jnp.clip(jax.random.normal(noise_key, (DG, DH), jnp.float32), -4.0, 4.0)
    trend = math.log(3.0)
    position = jnp.arange(DG, dtype=jnp.float32).reshape(DG, 1) / (DG - 1)
    rough = jax.random.uniform(scale_key, (DG, 1), jnp.float32, 0.0, math.log(4.0))
    scale = jnp.exp(trend * position + rough) / math.sqrt(DH)
    return jnp.clip(base * scale, -2.0, 2.0).astype(jnp.bfloat16)


def draw_clip_head(key, part):
    key = jax.random.fold_in(key, 32)
    noise_key, scale_key = jax.random.split(key)
    base = jnp.clip(jax.random.normal(noise_key, (DC, DH), jnp.float32), -4.0, 4.0)
    trend = math.log(3.0)
    position = jnp.arange(DC, dtype=jnp.float32).reshape(DC, 1) / (DC - 1)
    rough = jax.random.uniform(scale_key, (DC, 1), jnp.float32, 0.0, math.log(4.0))
    scale = jnp.exp(trend * position + rough) / math.sqrt(DH)
    return jnp.clip(base * scale, -2.0, 2.0).astype(jnp.bfloat16)


def steps_of(rng, extent, shards, low, high):
    loudness = 1.0
    for dim, parts in shards:
        heights = jax.random.uniform(jax.random.fold_in(jax.random.fold_in(rng, 6), dim), (parts,), jnp.float32, low / len(shards), high / len(shards))
        loudness = loudness * jnp.repeat(jnp.exp(heights), extent[dim] // parts).reshape((-1,) + (1,) * (len(extent) - 1 - dim))
    return loudness


def gaussian(own_key, shape, scale, limit, cuts=(), kind=jnp.bfloat16):
    array = jax.random.normal(own_key, shape, jnp.float32) * scale
    if len(cuts) > 0:
        array = steps_of(own_key, shape, cuts, -0.22, 0.18) * array
    return jnp.clip(array, min=-limit, max=limit).astype(kind)


def setup_inputs(seed: int = 0, part: int = 0) -> dict:
    key_list = jax.random.split(jax.random.key(seed), 12)
    own_keys = jax.random.split(jax.random.fold_in(key_list[11], part), 12)
    return {
        "giant_context": draw_giant_context(jax.random.fold_in(jax.random.fold_in(key_list[11], part), 71), part),
        "clip_context": draw_clip_context(jax.random.fold_in(jax.random.fold_in(key_list[11], part), 71), part),
        "giant_out": draw_giant_out(jax.random.fold_in(key_list[11], 71), part),
        "clip_out": draw_clip_out(jax.random.fold_in(key_list[11], 71), part),
        "giant_gain": jnp.clip(1.0 + 0.1 * jax.random.normal(key_list[4], (DG,), jnp.float32), 0.5, 1.5),
        "clip_gain": jnp.clip(1.0 + 0.1 * jax.random.normal(key_list[5], (DC,), jnp.float32), 0.5, 1.5),
        "student_features": gaussian(own_keys[6], (TOKENS, DS), 1.0, 6.0, ((0, 4),)),
        "giant_first": gaussian(key_list[7], (DH, DS), DS ** -0.5, 0.15625, ((0, 4),)),
        "clip_first": gaussian(key_list[8], (DH, DS), DS ** -0.5, 0.15625, ((0, 4),)),
        "giant_head": draw_giant_head(jax.random.fold_in(key_list[11], 71), part),
        "clip_head": draw_clip_head(jax.random.fold_in(key_list[11], 71), part),
    }


EPSILON = 1e-06
CONTRACT_FIRST = (((0,), (0,)), ((), ()))
CONTRACT_LAST = (((1,), (1,)), ((), ()))

def normal_cdf(values):
    return 0.5 * (1.0 + lax.erf(values * (1.0 / math.sqrt(2.0))))

def gelu_value(values):
    return values * normal_cdf(values)

def gelu_slope(values):
    return normal_cdf(values) + values * jnp.exp(-0.5 * values * values) * (1.0 / math.sqrt(2.0 * math.pi))

def teacher_target(context, weight, gain):
    width = weight.shape[1]
    block = context.shape[0] // N_TP
    context_blocks = context.reshape(N_TP, block, context.shape[1])
    weight_blocks = weight.reshape(N_TP, block, width)

    def add_block(total, pair):
        product = lax.dot_general(pair[1], pair[0], CONTRACT_FIRST, preferred_element_type=jnp.float32)
        rounded = lax.optimization_barrier(product.astype(jnp.bfloat16))
        return (total + rounded.astype(jnp.float32), None)
    start_total = jnp.zeros((width, context.shape[1]), jnp.float32)
    summed, _ = lax.scan(add_block, start_total, (context_blocks, weight_blocks))
    average = lax.optimization_barrier(jnp.mean(summed, axis=0))
    variance = lax.optimization_barrier(jnp.mean(summed * summed, axis=0)) - average * average
    inverse = lax.rsqrt(variance + EPSILON)
    return gain[:, None] * (summed - average) * inverse

def adaptor_grads(first, head, features, target):
    width = head.shape[0]
    pre = lax.dot_general(features, first, CONTRACT_LAST, preferred_element_type=jnp.float32)
    hidden = gelu_value(pre).astype(jnp.bfloat16)
    predicted = lax.dot_general(head, hidden, CONTRACT_LAST, preferred_element_type=jnp.float32)
    inner = lax.optimization_barrier(jnp.sum(predicted * target, axis=0))
    pred_sq = lax.optimization_barrier(jnp.sum(predicted * predicted, axis=0))
    target_sq = lax.optimization_barrier(jnp.sum(target * target, axis=0))
    inv_pred = lax.rsqrt(pred_sq + EPSILON)
    inv_target = lax.rsqrt(target_sq + EPSILON)
    cosine = inner * inv_pred * inv_target
    weight = width / 8.0
    slope = -weight * (target * (inv_pred * inv_target) - predicted * (cosine * inv_pred * inv_pred))
    slope = slope.astype(jnp.bfloat16)
    second_grad = jnp.dot(slope, hidden, preferred_element_type=jnp.float32)
    hidden_slope = lax.dot_general(head, slope, CONTRACT_FIRST, preferred_element_type=jnp.float32)
    pre_slope = (hidden_slope * gelu_slope(pre.T)).astype(jnp.bfloat16)
    first_grad = jnp.dot(pre_slope, features, preferred_element_type=jnp.float32)
    feature_term = lax.dot_general(pre_slope, first, CONTRACT_FIRST, preferred_element_type=jnp.float32)
    return (second_grad, first_grad, feature_term)

def reference(giant_context, clip_context, giant_out, clip_out, giant_gain, clip_gain, student_features, giant_first, clip_first, giant_head, clip_head):
    giant_target = teacher_target(giant_context, giant_out, giant_gain)
    clip_target = teacher_target(clip_context, clip_out, clip_gain)
    giant_second, giant_one, giant_term = adaptor_grads(giant_first, giant_head, student_features, giant_target)
    clip_second, clip_one, clip_term = adaptor_grads(clip_first, clip_head, student_features, clip_target)
    feature_term = giant_term + clip_term
    return (giant_second.astype(jnp.bfloat16), clip_second.astype(jnp.bfloat16), giant_one.astype(jnp.bfloat16), clip_one.astype(jnp.bfloat16), feature_term.astype(jnp.bfloat16))
```

```python
import math

import jax
import jax.numpy as jnp
from jax import lax
from jax.sharding import PartitionSpec as P

EPSILON = 1e-06
CONTRACT_FIRST = (((0,), (0,)), ((), ()))
CONTRACT_LAST = (((1,), (1,)), ((), ()))


def normal_cdf(values):
    return 0.5 * (1.0 + lax.erf(values * (1.0 / math.sqrt(2.0))))


def gelu_value(values):
    return values * normal_cdf(values)


def gelu_slope(values):
    return normal_cdf(values) + values * jnp.exp(-0.5 * values * values) * (
        1.0 / math.sqrt(2.0 * math.pi)
    )


def project_teacher(weight_rows, context):
    return lax.dot_general(weight_rows, context, CONTRACT_FIRST, preferred_element_type=jnp.float32)


def token_sums(own, gain_rows, predicted):
    gain = gain_rows[:, None]
    scaled = gain * own
    return jnp.stack(
        (
            jnp.sum(own, axis=0),
            jnp.sum(own * own, axis=0),
            jnp.sum(predicted * predicted, axis=0),
            jnp.sum(scaled * predicted, axis=0),
            jnp.sum(gain * predicted, axis=0),
            jnp.sum(scaled * scaled, axis=0),
            jnp.sum(gain * scaled, axis=0),
            jnp.broadcast_to(jnp.sum(gain * gain), own.shape[1:]),
        )
    )


def make_slope(own, gain_rows, predicted, sums, width):
    average = sums[0] / width
    inverse = lax.rsqrt(sums[1] / width - average * average + EPSILON)
    pred_sq = sums[2]
    inner = inverse * (sums[3] - average * sums[4])
    target_sq = inverse * inverse * (
        sums[5] - 2.0 * average * sums[6] + average * average * sums[7]
    )
    inv_pred = lax.rsqrt(pred_sq + EPSILON)
    inv_target = lax.rsqrt(target_sq + EPSILON)
    cosine = inner * inv_pred * inv_target
    weight = width / 8.0
    target = gain_rows[:, None] * (own - average) * inverse
    slope = -weight * (
        target * (inv_pred * inv_target) - predicted * (cosine * inv_pred * inv_pred)
    )
    return slope.astype(jnp.bfloat16)


def local(
    giant_context,
    clip_context,
    giant_out,
    clip_out,
    giant_gain,
    clip_gain,
    student_features,
    giant_first,
    clip_first,
    giant_head,
    clip_head,
):
    giant_width = giant_out.shape[1]
    clip_width = clip_out.shape[1]
    giant_pre = lax.dot_general(
        student_features, giant_first, CONTRACT_LAST, preferred_element_type=jnp.float32
    )
    clip_pre = lax.dot_general(
        student_features, clip_first, CONTRACT_LAST, preferred_element_type=jnp.float32
    )
    giant_hidden_own = gelu_value(giant_pre).astype(jnp.bfloat16)
    clip_hidden_own = gelu_value(clip_pre).astype(jnp.bfloat16)
    giant_hidden, clip_hidden = (
        lax.all_gather(giant_hidden_own, "tp", axis=1, tiled=True),
        lax.all_gather(clip_hidden_own, "tp", axis=1, tiled=True),
    )
    giant_pred = lax.dot_general(
        giant_head, giant_hidden, CONTRACT_LAST, preferred_element_type=jnp.float32
    )
    clip_pred = lax.dot_general(
        clip_head, clip_hidden, CONTRACT_LAST, preferred_element_type=jnp.float32
    )
    giant_own = lax.psum_scatter(
        project_teacher(giant_out, giant_context).astype(jnp.bfloat16),
        "tp",
        scatter_dimension=0,
        tiled=True,
    ).astype(jnp.float32)
    clip_own = lax.psum_scatter(
        project_teacher(clip_out, clip_context).astype(jnp.bfloat16),
        "tp",
        scatter_dimension=0,
        tiled=True,
    ).astype(jnp.float32)
    giant_stats, clip_stats = lax.psum(
        (
            token_sums(giant_own, giant_gain, giant_pred),
            token_sums(clip_own, clip_gain, clip_pred),
        ),
        "tp",
    )
    giant_slope = make_slope(giant_own, giant_gain, giant_pred, giant_stats, giant_width)
    clip_slope = make_slope(clip_own, clip_gain, clip_pred, clip_stats, clip_width)
    giant_second = jnp.dot(giant_slope, giant_hidden, preferred_element_type=jnp.float32)
    clip_second = jnp.dot(clip_slope, clip_hidden, preferred_element_type=jnp.float32)
    giant_hslope = lax.psum_scatter(
        lax.dot_general(
            giant_head, giant_slope, CONTRACT_FIRST, preferred_element_type=jnp.float32
        ).astype(jnp.bfloat16),
        "tp",
        scatter_dimension=0,
        tiled=True,
    ).astype(jnp.float32)
    clip_hslope = lax.psum_scatter(
        lax.dot_general(
            clip_head, clip_slope, CONTRACT_FIRST, preferred_element_type=jnp.float32
        ).astype(jnp.bfloat16),
        "tp",
        scatter_dimension=0,
        tiled=True,
    ).astype(jnp.float32)
    giant_pslope = (giant_hslope * gelu_slope(giant_pre.T)).astype(jnp.bfloat16)
    clip_pslope = (clip_hslope * gelu_slope(clip_pre.T)).astype(jnp.bfloat16)
    giant_one = jnp.dot(giant_pslope, student_features, preferred_element_type=jnp.float32)
    clip_one = jnp.dot(clip_pslope, student_features, preferred_element_type=jnp.float32)
    feature_term = lax.dot_general(
        giant_pslope, giant_first, CONTRACT_FIRST, preferred_element_type=jnp.float32
    )
    feature_term = feature_term + lax.dot_general(
        clip_pslope, clip_first, CONTRACT_FIRST, preferred_element_type=jnp.float32
    )
    feature_sum = lax.psum(feature_term.astype(jnp.bfloat16), "tp")
    giant_grad, clip_grad, giant_first_grad, clip_first_grad = (
        lax.psum_scatter(
            giant_second.astype(jnp.bfloat16), ("sec", "dp"), scatter_dimension=1, tiled=True
        ).astype(jnp.float32),
        lax.psum_scatter(
            clip_second.astype(jnp.bfloat16), ("sec", "dp"), scatter_dimension=1, tiled=True
        ).astype(jnp.float32),
        lax.psum_scatter(
            giant_one.astype(jnp.bfloat16), ("sec", "dp"), scatter_dimension=1, tiled=True
        ).astype(jnp.float32),
        lax.psum_scatter(
            clip_one.astype(jnp.bfloat16), ("sec", "dp"), scatter_dimension=1, tiled=True
        ).astype(jnp.float32),
    )
    return (
        giant_grad.astype(jnp.bfloat16),
        clip_grad.astype(jnp.bfloat16),
        giant_first_grad.astype(jnp.bfloat16),
        clip_first_grad.astype(jnp.bfloat16),
        feature_sum,
    )


def solution(mesh):
    placed = (
        P("tp", ("groups", "sec", "dp")),
        P("tp", ("groups", "sec", "dp")),
        P("tp", None),
        P("tp", None),
        P("tp"),
        P("tp"),
        P(("groups", "sec", "dp"), None),
        P("tp", None),
        P("tp", None),
        P("tp", None),
        P("tp", None),
    )
    return jax.shard_map(
        local,
        mesh=mesh,
        in_specs=placed,
        out_specs=(
            P(("groups", "tp"), ("sec", "dp")),
            P(("groups", "tp"), ("sec", "dp")),
            P(("groups", "tp"), ("sec", "dp")),
            P(("groups", "tp"), ("sec", "dp")),
            P(("groups", "sec", "dp"), None),
        ),
        check_vma=False,
    )
```

```python
import math

import jax
import jax.numpy as jnp
from jax import lax
from jax.sharding import PartitionSpec as P

EPSILON = 1e-06
CONTRACT_FIRST = (((0,), (0,)), ((), ()))
CONTRACT_LAST = (((1,), (1,)), ((), ()))


def normal_cdf(values):
    return 0.5 * (1.0 + lax.erf(values * (1.0 / math.sqrt(2.0))))


def gelu_value(values):
    return values * normal_cdf(values)


def gelu_slope(values):
    return normal_cdf(values) + values * jnp.exp(-0.5 * values * values) * (
        1.0 / math.sqrt(2.0 * math.pi)
    )


def project_teacher(weight_rows, context):
    return lax.dot_general(weight_rows, context, CONTRACT_FIRST, preferred_element_type=jnp.float32)


def token_sums(own, gain_rows, predicted):
    gain = gain_rows[:, None]
    scaled = gain * own
    return jnp.stack(
        (
            jnp.sum(own, axis=0),
            jnp.sum(own * own, axis=0),
            jnp.sum(predicted * predicted, axis=0),
            jnp.sum(scaled * predicted, axis=0),
            jnp.sum(gain * predicted, axis=0),
            jnp.sum(scaled * scaled, axis=0),
            jnp.sum(gain * scaled, axis=0),
            jnp.broadcast_to(jnp.sum(gain * gain), own.shape[1:]),
        )
    )


def make_slope(own, gain_rows, predicted, sums, width):
    average = sums[0] / width
    inverse = lax.rsqrt(sums[1] / width - average * average + EPSILON)
    pred_sq = sums[2]
    inner = inverse * (sums[3] - average * sums[4])
    target_sq = inverse * inverse * (
        sums[5] - 2.0 * average * sums[6] + average * average * sums[7]
    )
    inv_pred = lax.rsqrt(pred_sq + EPSILON)
    inv_target = lax.rsqrt(target_sq + EPSILON)
    cosine = inner * inv_pred * inv_target
    weight = width / 8.0
    target = gain_rows[:, None] * (own - average) * inverse
    slope = -weight * (
        target * (inv_pred * inv_target) - predicted * (cosine * inv_pred * inv_pred)
    )
    return slope.astype(jnp.bfloat16)


def tp_shift(value, step):
    count = lax.axis_size("tp")
    return lax.ppermute(value, "tp", [(i, (i + step) % count) for i in range(count)])


def tp_sum(value):
    count = lax.axis_size("tp")
    parts = [tp_shift(value, step) for step in range(1, count)]
    own = lax.axis_index("tp")
    stacked = jnp.zeros((count,) + value.shape, value.dtype)
    stacked = lax.dynamic_update_index_in_dim(stacked, value, own, 0)
    for step, part in enumerate(parts, 1):
        stacked = lax.dynamic_update_index_in_dim(stacked, part, (own - step) % count, 0)
    return jnp.sum(stacked, axis=0)


def tp_columns(value):
    count = lax.axis_size("tp")
    share = value.shape[1]
    own = lax.axis_index("tp")
    parts = [value] + [tp_shift(value, step) for step in range(1, count)]
    full = jnp.zeros((value.shape[0], share * count), value.dtype)
    for step, part in enumerate(parts):
        full = lax.dynamic_update_slice_in_dim(full, part, ((own - step) % count) * share, 1)
    return full


def summed_product(left, right):
    sections, cores = lax.axis_size("sec"), lax.axis_size("dp")
    if sections != 2 or cores != 2:
        product = jnp.dot(left, right, preferred_element_type=jnp.float32)
        return lax.psum_scatter(
            product.astype(jnp.bfloat16), ("sec", "dp"), scatter_dimension=1, tiled=True
        )
    share = right.shape[1] // 4
    sec, core = lax.axis_index("sec"), lax.axis_index("dp")
    swap = [(0, 1), (1, 0)]

    def piece(section, which):
        columns = lax.dynamic_slice_in_dim(right, (section * 2 + which) * share, share, 1)
        return jnp.dot(left, columns, preferred_element_type=jnp.float32)

    far = lax.ppermute(piece(1 - sec, 1 - core).astype(jnp.bfloat16), "dp", swap)
    near = lax.ppermute(piece(sec, 1 - core).astype(jnp.bfloat16), "dp", swap)
    other = lax.ppermute(
        (piece(1 - sec, core) + far.astype(jnp.float32)).astype(jnp.bfloat16), "sec", swap
    )
    total = piece(sec, core) + near.astype(jnp.float32) + other.astype(jnp.float32)
    return total.astype(jnp.bfloat16)


def own_rows(weight_rows, context):
    return lax.psum_scatter(
        project_teacher(weight_rows, context).astype(jnp.bfloat16),
        "tp",
        scatter_dimension=0,
        tiled=True,
    ).astype(jnp.float32)


def local(
    giant_context,
    clip_context,
    giant_out,
    clip_out,
    giant_gain,
    clip_gain,
    student_features,
    giant_first,
    clip_first,
    giant_head,
    clip_head,
):
    giant_width = giant_out.shape[1]
    clip_width = clip_out.shape[1]
    clip_own = own_rows(clip_out, clip_context)
    giant_own = own_rows(giant_out, giant_context)
    clip_pre = lax.dot_general(
        student_features, clip_first, CONTRACT_LAST, preferred_element_type=jnp.float32
    )
    giant_pre = lax.dot_general(
        student_features, giant_first, CONTRACT_LAST, preferred_element_type=jnp.float32
    )
    clip_hidden = tp_columns(gelu_value(clip_pre).astype(jnp.bfloat16))
    giant_hidden = tp_columns(gelu_value(giant_pre).astype(jnp.bfloat16))
    clip_pred = lax.dot_general(
        clip_head, clip_hidden, CONTRACT_LAST, preferred_element_type=jnp.float32
    )
    giant_pred = lax.dot_general(
        giant_head, giant_hidden, CONTRACT_LAST, preferred_element_type=jnp.float32
    )
    clip_stats = tp_sum(token_sums(clip_own, clip_gain, clip_pred))
    clip_slope = make_slope(clip_own, clip_gain, clip_pred, clip_stats, clip_width)
    clip_grad = summed_product(clip_slope, clip_hidden)
    clip_back = lax.dot_general(
        clip_head, clip_slope, CONTRACT_FIRST, preferred_element_type=jnp.float32
    ).astype(jnp.bfloat16)
    giant_stats = tp_sum(token_sums(giant_own, giant_gain, giant_pred))
    giant_slope = make_slope(giant_own, giant_gain, giant_pred, giant_stats, giant_width)
    giant_back = lax.dot_general(
        giant_head, giant_slope, CONTRACT_FIRST, preferred_element_type=jnp.float32
    ).astype(jnp.bfloat16)
    back = lax.psum_scatter(
        jnp.concatenate((giant_back, clip_back), axis=1), "tp", scatter_dimension=0, tiled=True
    ).astype(jnp.float32)
    giant_grad = summed_product(giant_slope, giant_hidden)
    tokens = student_features.shape[0]
    giant_pslope = (back[:, :tokens] * gelu_slope(giant_pre.T)).astype(jnp.bfloat16)
    clip_pslope = (back[:, tokens:] * gelu_slope(clip_pre.T)).astype(jnp.bfloat16)
    feature_term = lax.dot_general(
        giant_pslope, giant_first, CONTRACT_FIRST, preferred_element_type=jnp.float32
    )
    feature_term = feature_term + lax.dot_general(
        clip_pslope, clip_first, CONTRACT_FIRST, preferred_element_type=jnp.float32
    )
    feature_sum = lax.psum(feature_term.astype(jnp.bfloat16), "tp")
    giant_first_grad = summed_product(giant_pslope, student_features)
    clip_first_grad = summed_product(clip_pslope, student_features)
    return (giant_grad, clip_grad, giant_first_grad, clip_first_grad, feature_sum)


def solution(mesh):
    placed = (
        P("tp", ("groups", "sec", "dp")),
        P("tp", ("groups", "sec", "dp")),
        P("tp", None),
        P("tp", None),
        P("tp"),
        P("tp"),
        P(("groups", "sec", "dp"), None),
        P("tp", None),
        P("tp", None),
        P("tp", None),
        P("tp", None),
    )
    return jax.shard_map(
        local,
        mesh=mesh,
        in_specs=placed,
        out_specs=(
            P(("groups", "tp"), ("sec", "dp")),
            P(("groups", "tp"), ("sec", "dp")),
            P(("groups", "tp"), ("sec", "dp")),
            P(("groups", "tp"), ("sec", "dp")),
            P(("groups", "sec", "dp"), None),
        ),
        check_vma=False,
    )
```

```python
import math

import jax
import jax.numpy as jnp
from jax import lax
from jax.sharding import PartitionSpec as P

EPSILON = 1e-06
CONTRACT_FIRST = (((0,), (0,)), ((), ()))
CONTRACT_LAST = (((1,), (1,)), ((), ()))


def normal_cdf(values):
    return 0.5 * (1.0 + lax.erf(values * (1.0 / math.sqrt(2.0))))


def gelu_value(values):
    return values * normal_cdf(values)


def gelu_slope(values):
    return normal_cdf(values) + values * jnp.exp(-0.5 * values * values) * (
        1.0 / math.sqrt(2.0 * math.pi)
    )


def project_teacher(weight_rows, context):
    return lax.dot_general(weight_rows, context, CONTRACT_FIRST, preferred_element_type=jnp.float32)


def token_sums(own, gain_rows, predicted):
    gain = gain_rows[:, None]
    scaled = gain * own
    return jnp.stack(
        (
            jnp.sum(own, axis=0),
            jnp.sum(own * own, axis=0),
            jnp.sum(predicted * predicted, axis=0),
            jnp.sum(scaled * predicted, axis=0),
            jnp.sum(gain * predicted, axis=0),
            jnp.sum(scaled * scaled, axis=0),
            jnp.sum(gain * scaled, axis=0),
            jnp.broadcast_to(jnp.sum(gain * gain), own.shape[1:]),
        )
    )


def make_slope(own, gain_rows, predicted, sums, width):
    average = sums[0] / width
    inverse = lax.rsqrt(sums[1] / width - average * average + EPSILON)
    pred_sq = sums[2]
    inner = inverse * (sums[3] - average * sums[4])
    target_sq = inverse * inverse * (
        sums[5] - 2.0 * average * sums[6] + average * average * sums[7]
    )
    inv_pred = lax.rsqrt(pred_sq + EPSILON)
    inv_target = lax.rsqrt(target_sq + EPSILON)
    cosine = inner * inv_pred * inv_target
    weight = width / 8.0
    target = gain_rows[:, None] * (own - average) * inverse
    slope = -weight * (
        target * (inv_pred * inv_target) - predicted * (cosine * inv_pred * inv_pred)
    )
    return slope.astype(jnp.bfloat16)


def tp_shift(value, step):
    count = lax.axis_size("tp")
    return lax.ppermute(value, "tp", [(i, (i + step) % count) for i in range(count)])


def tp_sum(value):
    count = lax.axis_size("tp")
    parts = [tp_shift(value, step) for step in range(1, count)]
    own = lax.axis_index("tp")
    stacked = jnp.zeros((count,) + value.shape, value.dtype)
    stacked = lax.dynamic_update_index_in_dim(stacked, value, own, 0)
    for step, part in enumerate(parts, 1):
        stacked = lax.dynamic_update_index_in_dim(stacked, part, (own - step) % count, 0)
    return jnp.sum(stacked, axis=0)


def tp_columns(value):
    count = lax.axis_size("tp")
    share = value.shape[1]
    own = lax.axis_index("tp")
    parts = [value] + [tp_shift(value, step) for step in range(1, count)]
    full = jnp.zeros((value.shape[0], share * count), value.dtype)
    for step, part in enumerate(parts):
        full = lax.dynamic_update_slice_in_dim(full, part, ((own - step) % count) * share, 1)
    return full


def summed_product(left, right, after=None):
    sections, cores = lax.axis_size("sec"), lax.axis_size("dp")
    if sections != 2 or cores != 2:
        product = jnp.dot(left, right, preferred_element_type=jnp.float32)
        return lax.psum_scatter(
            product.astype(jnp.bfloat16), ("sec", "dp"), scatter_dimension=1, tiled=True
        )
    share = right.shape[1] // 4
    sec, core = lax.axis_index("sec"), lax.axis_index("dp")
    swap = [(0, 1), (1, 0)]

    def piece(section, which):
        columns = lax.dynamic_slice_in_dim(right, (section * 2 + which) * share, share, 1)
        return jnp.dot(left, columns, preferred_element_type=jnp.float32)

    far = lax.ppermute(piece(1 - sec, 1 - core).astype(jnp.bfloat16), "dp", swap)
    near = lax.ppermute(piece(sec, 1 - core).astype(jnp.bfloat16), "dp", swap)
    outgoing = (piece(1 - sec, core) + far.astype(jnp.float32)).astype(jnp.bfloat16)
    if after is not None:
        outgoing, _ = lax.optimization_barrier((outgoing, after))
    other = lax.ppermute(outgoing, "sec", swap)
    total = piece(sec, core) + near.astype(jnp.float32) + other.astype(jnp.float32)
    return total.astype(jnp.bfloat16)


def own_rows(weight_rows, context):
    return lax.psum_scatter(
        project_teacher(weight_rows, context).astype(jnp.bfloat16),
        "tp",
        scatter_dimension=0,
        tiled=True,
    )


def local(
    giant_context,
    clip_context,
    giant_out,
    clip_out,
    giant_gain,
    clip_gain,
    student_features,
    giant_first,
    clip_first,
    giant_head,
    clip_head,
):
    giant_width = giant_out.shape[1]
    clip_width = clip_out.shape[1]
    clip_own = own_rows(clip_out, clip_context)
    giant_own = own_rows(giant_out, giant_context)
    clip_pre = lax.dot_general(
        student_features, clip_first, CONTRACT_LAST, preferred_element_type=jnp.float32
    )
    giant_pre = lax.dot_general(
        student_features, giant_first, CONTRACT_LAST, preferred_element_type=jnp.float32
    )
    clip_hidden = tp_columns(gelu_value(clip_pre).astype(jnp.bfloat16))
    giant_hidden = tp_columns(gelu_value(giant_pre).astype(jnp.bfloat16))
    clip_pred = lax.dot_general(
        clip_head, clip_hidden, CONTRACT_LAST, preferred_element_type=jnp.float32
    )
    giant_pred = lax.dot_general(
        giant_head, giant_hidden, CONTRACT_LAST, preferred_element_type=jnp.float32
    )
    clip_stats = tp_sum(token_sums(clip_own.astype(jnp.float32), clip_gain, clip_pred))
    clip_slope = make_slope(clip_own.astype(jnp.float32), clip_gain, clip_pred, clip_stats, clip_width)
    clip_grad = summed_product(clip_slope, clip_hidden)
    clip_back = lax.dot_general(
        clip_head, clip_slope, CONTRACT_FIRST, preferred_element_type=jnp.float32
    ).astype(jnp.bfloat16)
    giant_own, clip_grad, clip_back = lax.optimization_barrier((giant_own, clip_grad, clip_back))
    giant_stats = tp_sum(token_sums(giant_own.astype(jnp.float32), giant_gain, giant_pred))
    giant_slope = make_slope(giant_own.astype(jnp.float32), giant_gain, giant_pred, giant_stats, giant_width)
    giant_back = lax.dot_general(
        giant_head, giant_slope, CONTRACT_FIRST, preferred_element_type=jnp.float32
    ).astype(jnp.bfloat16)
    back = lax.psum_scatter(
        jnp.concatenate((giant_back, clip_back), axis=1), "tp", scatter_dimension=0, tiled=True
    ).astype(jnp.float32)
    tokens = student_features.shape[0]
    giant_pslope = (back[:, :tokens] * gelu_slope(giant_pre.T)).astype(jnp.bfloat16)
    clip_pslope = (back[:, tokens:] * gelu_slope(clip_pre.T)).astype(jnp.bfloat16)
    feature_term = lax.dot_general(
        giant_pslope, giant_first, CONTRACT_FIRST, preferred_element_type=jnp.float32
    )
    feature_term = feature_term + lax.dot_general(
        clip_pslope, clip_first, CONTRACT_FIRST, preferred_element_type=jnp.float32
    )
    feature_term = feature_term.astype(jnp.bfloat16)
    feature_sum = lax.psum(feature_term, "tp")
    giant_grad = summed_product(giant_slope, giant_hidden, after=feature_term)
    giant_first_grad = summed_product(giant_pslope, student_features)
    clip_first_grad = summed_product(clip_pslope, student_features)
    return (giant_grad, clip_grad, giant_first_grad, clip_first_grad, feature_sum)


def solution(mesh):
    placed = (
        P("tp", ("groups", "sec", "dp")),
        P("tp", ("groups", "sec", "dp")),
        P("tp", None),
        P("tp", None),
        P("tp"),
        P("tp"),
        P(("groups", "sec", "dp"), None),
        P("tp", None),
        P("tp", None),
        P("tp", None),
        P("tp", None),
    )
    return jax.shard_map(
        local,
        mesh=mesh,
        in_specs=placed,
        out_specs=(
            P(("groups", "tp"), ("sec", "dp")),
            P(("groups", "tp"), ("sec", "dp")),
            P(("groups", "tp"), ("sec", "dp")),
            P(("groups", "tp"), ("sec", "dp")),
            P(("groups", "sec", "dp"), None),
        ),
        check_vma=False,
    )
```

```python
import math

import jax
import jax.numpy as jnp
from jax import lax
from jax.sharding import PartitionSpec as P

EPSILON = 1e-06
CONTRACT_FIRST = (((0,), (0,)), ((), ()))
CONTRACT_LAST = (((1,), (1,)), ((), ()))


def normal_cdf(values):
    return 0.5 * (1.0 + lax.erf(values * (1.0 / math.sqrt(2.0))))


def gelu_value(values):
    return values * normal_cdf(values)


def gelu_slope(values):
    return normal_cdf(values) + values * jnp.exp(-0.5 * values * values) * (
        1.0 / math.sqrt(2.0 * math.pi)
    )


def project_teacher(weight_rows, context):
    return lax.dot_general(weight_rows, context, CONTRACT_FIRST, preferred_element_type=jnp.float32)


def token_sums(own, gain_rows, predicted):
    gain = gain_rows[:, None]
    scaled = gain * own
    return jnp.stack(
        (
            jnp.sum(own, axis=0),
            jnp.sum(own * own, axis=0),
            jnp.sum(predicted * predicted, axis=0),
            jnp.sum(scaled * predicted, axis=0),
            jnp.sum(gain * predicted, axis=0),
            jnp.sum(scaled * scaled, axis=0),
            jnp.sum(gain * scaled, axis=0),
            jnp.broadcast_to(jnp.sum(gain * gain), own.shape[1:]),
        )
    )


def make_slope(own, gain_rows, predicted, sums, width):
    average = sums[0] / width
    inverse = lax.rsqrt(sums[1] / width - average * average + EPSILON)
    pred_sq = sums[2]
    inner = inverse * (sums[3] - average * sums[4])
    target_sq = inverse * inverse * (
        sums[5] - 2.0 * average * sums[6] + average * average * sums[7]
    )
    inv_pred = lax.rsqrt(pred_sq + EPSILON)
    inv_target = lax.rsqrt(target_sq + EPSILON)
    cosine = inner * inv_pred * inv_target
    weight = width / 8.0
    target = gain_rows[:, None] * (own - average) * inverse
    slope = -weight * (
        target * (inv_pred * inv_target) - predicted * (cosine * inv_pred * inv_pred)
    )
    return slope.astype(jnp.bfloat16)


def tp_shift(value, step):
    count = lax.axis_size("tp")
    return lax.ppermute(value, "tp", [(i, (i + step) % count) for i in range(count)])


def tp_sum(value):
    count = lax.axis_size("tp")
    parts = [tp_shift(value, step) for step in range(1, count)]
    own = lax.axis_index("tp")
    stacked = jnp.zeros((count,) + value.shape, value.dtype)
    stacked = lax.dynamic_update_index_in_dim(stacked, value, own, 0)
    for step, part in enumerate(parts, 1):
        stacked = lax.dynamic_update_index_in_dim(stacked, part, (own - step) % count, 0)
    return jnp.sum(stacked, axis=0)


def tp_columns(value):
    count = lax.axis_size("tp")
    share = value.shape[1]
    own = lax.axis_index("tp")
    parts = [value] + [tp_shift(value, step) for step in range(1, count)]
    full = jnp.zeros((value.shape[0], share * count), value.dtype)
    for step, part in enumerate(parts):
        full = lax.dynamic_update_slice_in_dim(full, part, ((own - step) % count) * share, 1)
    return full


def summed_product(left, right, after=None):
    sections, cores = lax.axis_size("sec"), lax.axis_size("dp")
    if sections != 2 or cores != 2:
        product = jnp.dot(left, right, preferred_element_type=jnp.float32)
        return lax.psum_scatter(
            product.astype(jnp.bfloat16), ("sec", "dp"), scatter_dimension=1, tiled=True
        )
    share = right.shape[1] // 4
    sec, core = lax.axis_index("sec"), lax.axis_index("dp")
    swap = [(0, 1), (1, 0)]

    def piece(section, which):
        columns = lax.dynamic_slice_in_dim(right, (section * 2 + which) * share, share, 1)
        return jnp.dot(left, columns, preferred_element_type=jnp.float32)

    far = lax.ppermute(piece(1 - sec, 1 - core).astype(jnp.bfloat16), "dp", swap)
    near = lax.ppermute(piece(sec, 1 - core).astype(jnp.bfloat16), "dp", swap)
    outgoing = (piece(1 - sec, core) + far.astype(jnp.float32)).astype(jnp.bfloat16)
    if after is not None:
        outgoing, _ = lax.optimization_barrier((outgoing, after))
    other = lax.ppermute(outgoing, "sec", swap)
    total = piece(sec, core) + near.astype(jnp.float32) + other.astype(jnp.float32)
    return total.astype(jnp.bfloat16)


def own_rows(weight_rows, context):
    return lax.psum_scatter(
        project_teacher(weight_rows, context).astype(jnp.bfloat16),
        "tp",
        scatter_dimension=0,
        tiled=True,
    )


def local(
    giant_context,
    clip_context,
    giant_out,
    clip_out,
    giant_gain,
    clip_gain,
    student_features,
    giant_first,
    clip_first,
    giant_head,
    clip_head,
):
    giant_width = giant_out.shape[1]
    clip_width = clip_out.shape[1]
    clip_own = own_rows(clip_out, clip_context)
    giant_own = own_rows(giant_out, giant_context)
    clip_pre = lax.dot_general(
        student_features, clip_first, CONTRACT_LAST, preferred_element_type=jnp.float32
    )
    giant_pre = lax.dot_general(
        student_features, giant_first, CONTRACT_LAST, preferred_element_type=jnp.float32
    )
    clip_hidden = tp_columns(gelu_value(clip_pre).astype(jnp.bfloat16))
    giant_hidden = tp_columns(gelu_value(giant_pre).astype(jnp.bfloat16))
    clip_pred = lax.dot_general(
        clip_head, clip_hidden, CONTRACT_LAST, preferred_element_type=jnp.float32
    )
    giant_pred = lax.dot_general(
        giant_head, giant_hidden, CONTRACT_LAST, preferred_element_type=jnp.float32
    )
    clip_stats = tp_sum(token_sums(clip_own.astype(jnp.float32), clip_gain, clip_pred))
    clip_slope = make_slope(clip_own.astype(jnp.float32), clip_gain, clip_pred, clip_stats, clip_width)
    clip_grad = summed_product(clip_slope, clip_hidden)
    clip_back = lax.dot_general(
        clip_head, clip_slope, CONTRACT_FIRST, preferred_element_type=jnp.float32
    ).astype(jnp.bfloat16)
    giant_own, clip_grad, clip_back = lax.optimization_barrier((giant_own, clip_grad, clip_back))
    clip_hslope = lax.psum_scatter(
        clip_back, "tp", scatter_dimension=0, tiled=True
    ).astype(jnp.float32)
    giant_stats = tp_sum(token_sums(giant_own.astype(jnp.float32), giant_gain, giant_pred))
    giant_slope = make_slope(giant_own.astype(jnp.float32), giant_gain, giant_pred, giant_stats, giant_width)
    giant_back = lax.dot_general(
        giant_head, giant_slope, CONTRACT_FIRST, preferred_element_type=jnp.float32
    ).astype(jnp.bfloat16)
    giant_hslope = lax.psum_scatter(
        giant_back, "tp", scatter_dimension=0, tiled=True
    ).astype(jnp.float32)
    giant_pslope = (giant_hslope * gelu_slope(giant_pre.T)).astype(jnp.bfloat16)
    clip_pslope = (clip_hslope * gelu_slope(clip_pre.T)).astype(jnp.bfloat16)
    feature_term = lax.dot_general(
        giant_pslope, giant_first, CONTRACT_FIRST, preferred_element_type=jnp.float32
    )
    feature_term = feature_term + lax.dot_general(
        clip_pslope, clip_first, CONTRACT_FIRST, preferred_element_type=jnp.float32
    )
    feature_term = feature_term.astype(jnp.bfloat16)
    feature_sum = lax.psum(feature_term, "tp")
    giant_grad = summed_product(giant_slope, giant_hidden, after=feature_term)
    giant_first_grad = summed_product(giant_pslope, student_features)
    clip_first_grad = summed_product(clip_pslope, student_features)
    return (giant_grad, clip_grad, giant_first_grad, clip_first_grad, feature_sum)


def solution(mesh):
    placed = (
        P("tp", ("groups", "sec", "dp")),
        P("tp", ("groups", "sec", "dp")),
        P("tp", None),
        P("tp", None),
        P("tp"),
        P("tp"),
        P(("groups", "sec", "dp"), None),
        P("tp", None),
        P("tp", None),
        P("tp", None),
        P("tp", None),
    )
    return jax.shard_map(
        local,
        mesh=mesh,
        in_specs=placed,
        out_specs=(
            P(("groups", "tp"), ("sec", "dp")),
            P(("groups", "tp"), ("sec", "dp")),
            P(("groups", "tp"), ("sec", "dp")),
            P(("groups", "tp"), ("sec", "dp")),
            P(("groups", "sec", "dp"), None),
        ),
        check_vma=False,
    )
```
